32 devices in a mesh: seq: 8 (over z, y), chan: 4 (over x, core).
Axes of the slice: x: 2, y: 2, z: 4, core: 2. Of those that a mesh axis runs over, the one named last changes fastest.
Arguments:
- outer_gate: bfloat16 [256, 262144], P('chan', 'seq'), may hold values from -6 to 6
- inner_gate: bfloat16 [256, 262144], P('chan', 'seq'), may hold values from -6 to 6
- signal: bfloat16 [256, 262144], P('chan', 'seq'), may hold values from -6 to 6
- filter_spectrum: float32 [2, 4, 512, 512], P(None, None, 'seq'), may hold values from -6 to 6
- cotangent: bfloat16 [256, 262144], P('chan', 'seq'), may hold values from -6 to 6
Outputs:
- output: bfloat16 [256, 262144], P('chan', 'seq')
- gradient_outer: bfloat16 [256, 262144], P('chan', 'seq')
- gradient_inner: bfloat16 [256, 262144], P('chan', 'seq')
- gradient_signal: bfloat16 [256, 262144], P('chan', 'seq')
- gradient_filter: float32 [2, 4, 512, 512], P(None, None, 'seq')
The draws below stay inside these ranges and needn't reach their ends.
All inputs are finite; a program needn't handle non-finite values.
Results may differ from the reference program's by a relative error of at most 0.018.
Values may be sent and summed in bfloat16 or wider, within the bound.
A program may use at most 256 MiB of HBM per device.

```python
import math
import jax
import jax.numpy as jnp
from jax import lax

FACTOR = 512
FILTERS = 4
LENGTH = 262144
CHANNELS = 256


def steps_of(own_key, extent, pieces, smallest, largest):
    loudness = 1.0
    for position, blocks in pieces:
        draws = jax.random.uniform(jax.random.fold_in(jax.random.fold_in(own_key, 6), position), (blocks,), jnp.float32, smallest / len(pieces), largest / len(pieces))
        loudness = loudness * jnp.repeat(jnp.exp(draws), extent[position] // blocks).reshape((-1,) + (1,) * (len(extent) - 1 - position))
    return loudness


def scatter_about(key, shape, deviation, limit, split=(), held_as=jnp.bfloat16):
    values = deviation * jax.random.normal(key, shape, jnp.float32)
    if split:
        values = values * steps_of(key, shape, split, -0.22, 0.18)
    return jnp.clip(values, -limit, limit).astype(held_as)


def setup_inputs(seed: int = 0) -> dict:
    splits = jax.random.split(jax.random.key(seed), 6)
    outer_gate = scatter_about(splits[0], (CHANNELS, LENGTH), 1.0, 6.0, ((0, 4), (1, 8)))
    inner_gate = scatter_about(splits[1], (CHANNELS, LENGTH), 1.0, 6.0, ((0, 4), (1, 8)))
    signal = scatter_about(splits[2], (CHANNELS, LENGTH), 1.0, 6.0, ((0, 4), (1, 8)))
    filter_spectrum = scatter_about(splits[3], (2, FILTERS, FACTOR, FACTOR), 1.0, 6.0, ((2, 8),), jnp.float32)
    cotangent = scatter_about(splits[4], (CHANNELS, LENGTH), 1.0, 6.0, ((0, 4), (1, 8)))
    return dict(outer_gate=outer_gate, inner_gate=inner_gate, signal=signal, filter_spectrum=filter_spectrum, cotangent=cotangent)


def rounded(value):
    narrow = lax.optimization_barrier(value.astype(jnp.bfloat16))
    return narrow.astype(jnp.float32)


def twiddle_grid():
    ordinal = jnp.arange(FACTOR, dtype=jnp.int32)
    phases = (ordinal[:, None] * ordinal[None, :]) % LENGTH
    angles = phases.astype(jnp.float32) * (2.0 * math.pi / LENGTH)
    return jnp.cos(angles), jnp.sin(angles)


def transform(source):
    square = source.astype(jnp.float32).reshape(source.shape[:-1] + (FACTOR, FACTOR))
    sectioned = jnp.fft.fft(square, axis=-2)
    wave_cos, wave_sin = twiddle_grid()
    twist_re = rounded(sectioned.real * wave_cos + sectioned.imag * wave_sin)
    twist_im = rounded(sectioned.imag * wave_cos - sectioned.real * wave_sin)
    spectrum = jnp.fft.fft(lax.complex(twist_re, twist_im), axis=-1)
    return spectrum.real, spectrum.imag


def restore(spectrum_re, spectrum_im):
    wave_cos, wave_sin = twiddle_grid()
    unwound = jnp.fft.ifft(lax.complex(spectrum_re, spectrum_im), axis=-1)
    untwist_re = rounded(unwound.real * wave_cos - unwound.imag * wave_sin)
    untwist_im = rounded(unwound.imag * wave_cos + unwound.real * wave_sin)
    values = jnp.fft.ifft(lax.complex(untwist_re, untwist_im), axis=-2).real
    return values.reshape(values.shape[:-2] + (LENGTH,)).astype(jnp.bfloat16)


def one_filter(grouped):
    mixed_rows, cotangent_rows, kernel = grouped
    forward_re, forward_im = transform(mixed_rows)
    backward_re, backward_im = transform(cotangent_rows)
    kernel_re = kernel[0]
    kernel_im = kernel[1]
    output_re = rounded(forward_re * kernel_re - forward_im * kernel_im)
    output_im = rounded(forward_re * kernel_im + forward_im * kernel_re)
    input_re = rounded(kernel_re * backward_re + kernel_im * backward_im)
    input_im = rounded(kernel_re * backward_im - kernel_im * backward_re)
    gradient_re = jnp.sum(forward_re * backward_re + forward_im * backward_im, axis=0) / LENGTH
    gradient_im = jnp.sum(forward_re * backward_im - forward_im * backward_re, axis=0) / LENGTH
    return restore(output_re, output_im), restore(input_re, input_im), jnp.stack([gradient_re, gradient_im])


def reference(outer_gate, inner_gate, signal, filter_spectrum, cotangent):
    mixed_input = (inner_gate.astype(jnp.float32) * signal.astype(jnp.float32)).astype(jnp.bfloat16)
    gated_cotangent = (cotangent.astype(jnp.float32) * outer_gate.astype(jnp.float32)).astype(jnp.bfloat16)
    mixed_groups = mixed_input.reshape(CHANNELS // FILTERS, FILTERS, LENGTH).transpose(1, 0, 2)
    cotangent_groups = gated_cotangent.reshape(CHANNELS // FILTERS, FILTERS, LENGTH).transpose(1, 0, 2)
    kernels = filter_spectrum.transpose(1, 0, 2, 3)
    long_groups, gradient_groups, filter_groups = lax.map(one_filter, (mixed_groups, cotangent_groups, kernels))
    long_output = long_groups.transpose(1, 0, 2).reshape(CHANNELS, LENGTH).astype(jnp.float32)
    mixed_gradient = gradient_groups.transpose(1, 0, 2).reshape(CHANNELS, LENGTH).astype(jnp.float32)
    output = (outer_gate.astype(jnp.float32) * long_output).astype(jnp.bfloat16)
    gradient_outer = (cotangent.astype(jnp.float32) * long_output).astype(jnp.bfloat16)
    gradient_inner = (mixed_gradient * signal.astype(jnp.float32)).astype(jnp.bfloat16)
    gradient_signal = (mixed_gradient * inner_gate.astype(jnp.float32)).astype(jnp.bfloat16)
    gradient_filter = filter_groups.transpose(1, 0, 2, 3)
    return output, gradient_outer, gradient_inner, gradient_signal, gradient_filter
```

```python
import functools
import math

import jax
import jax.numpy as jnp
from jax import lax
from jax.experimental import pallas as pl
from jax.experimental.pallas import tpu as pltpu
from jax.sharding import PartitionSpec as P

MESH = pl.DeviceIdType.MESH
VMEM_BYTES = 56 * 1024 * 1024


def wave_tables(factor):
    ordinal = jnp.arange(factor, dtype=jnp.int32)
    phases = ordinal[:, None] * ordinal[None, :] % factor
    angles = phases.astype(jnp.float32) * (2.0 * math.pi / factor)
    return (jnp.cos(angles).astype(jnp.bfloat16), jnp.sin(angles).astype(jnp.bfloat16))


def twist_grid(leading, second, length):
    phases = leading[:, None] * second[None, :] % length
    angles = phases.astype(jnp.float32) * (2.0 * math.pi / length)
    return (jnp.cos(angles), jnp.sin(angles))


def product(operand, pattern, matrix):
    return jnp.einsum(pattern, operand, matrix, preferred_element_type=jnp.float32)


def transform(stacked, spread, collect, tables, location, length):
    cos_table, sin_table = tables
    factor = cos_table.shape[0]
    received = spread(stacked)
    block_size = received.shape[3]
    columns = location * block_size + jnp.arange(block_size, dtype=jnp.int32)
    wave_cos, wave_sin = twist_grid(columns, jnp.arange(factor, dtype=jnp.int32), length)
    sectioned_re = product(received, "ncab,ak->ncbk", cos_table)
    sectioned_im = -product(received, "ncab,ak->ncbk", sin_table)
    twisted = jnp.stack(
        [
            sectioned_re * wave_cos + sectioned_im * wave_sin,
            sectioned_im * wave_cos - sectioned_re * wave_sin,
        ],
        axis=1,
    ).astype(jnp.bfloat16)
    arrived = collect(twisted)
    arrived_re = arrived[:, 0]
    arrived_im = arrived[:, 1]
    spectrum_re = product(arrived_re, "ncbk,bm->nckm", cos_table) + product(
        arrived_im, "ncbk,bm->nckm", sin_table
    )
    spectrum_im = product(arrived_im, "ncbk,bm->nckm", cos_table) - product(
        arrived_re, "ncbk,bm->nckm", sin_table
    )
    return (spectrum_re, spectrum_im)


def inverse(spectrum_re, spectrum_im, deliver, restore, tables, location, length):
    cos_table, sin_table = tables
    factor = cos_table.shape[0]
    shrink = 1.0 / factor
    block_size = spectrum_re.shape[2]
    row_ids = location * block_size + jnp.arange(block_size, dtype=jnp.int32)
    wave_cos, wave_sin = twist_grid(row_ids, jnp.arange(factor, dtype=jnp.int32), length)
    unwound_re = (
        product(spectrum_re, "nckm,mb->nckb", cos_table)
        - product(spectrum_im, "nckm,mb->nckb", sin_table)
    ) * shrink
    unwound_im = (
        product(spectrum_im, "nckm,mb->nckb", cos_table)
        + product(spectrum_re, "nckm,mb->nckb", sin_table)
    ) * shrink
    untwisted = jnp.stack(
        [
            unwound_re * wave_cos - unwound_im * wave_sin,
            unwound_im * wave_cos + unwound_re * wave_sin,
        ],
        axis=1,
    ).astype(jnp.bfloat16)
    arrived = deliver(untwisted)
    values = (
        (
            product(arrived[:, 0], "nckb,ka->ncab", cos_table)
            - product(arrived[:, 1], "nckb,ka->ncab", sin_table)
        )
        * shrink
    ).astype(jnp.bfloat16)
    return restore(values)


def grouped(values, kernel):
    return values.reshape((-1,) + kernel.shape)


def forward_product(forward_re, forward_im, kernel_re, kernel_im):
    shape = forward_re.shape
    front_re = grouped(forward_re, kernel_re)
    front_im = grouped(forward_im, kernel_re)
    output_re = (front_re * kernel_re - front_im * kernel_im).astype(jnp.bfloat16).reshape(shape)
    output_im = (front_re * kernel_im + front_im * kernel_re).astype(jnp.bfloat16).reshape(shape)
    return (output_re, output_im)


def backward_product(backward_re, backward_im, kernel_re, kernel_im):
    shape = backward_re.shape
    back_re = grouped(backward_re, kernel_re)
    back_im = grouped(backward_im, kernel_re)
    input_re = (kernel_re * back_re + kernel_im * back_im).astype(jnp.bfloat16).reshape(shape)
    input_im = (kernel_re * back_im - kernel_im * back_re).astype(jnp.bfloat16).reshape(shape)
    return (input_re, input_im)


def per_device(outer_gate, inner_gate, signal, filter_spectrum, cotangent):
    channels, positions = signal.shape
    factor = filter_spectrum.shape[3]
    length = factor * factor
    row_count = positions // factor
    location = lax.axis_index("seq")
    tables = wave_tables(factor)
    mixed_input = (
        (inner_gate.astype(jnp.float32) * signal.astype(jnp.float32))
        .astype(jnp.bfloat16)
        .reshape(channels, row_count, factor)
    )
    gated_cotangent = (
        (cotangent.astype(jnp.float32) * outer_gate.astype(jnp.float32))
        .astype(jnp.bfloat16)
        .reshape(channels, row_count, factor)
    )
    kernel_re = filter_spectrum[0]
    kernel_im = filter_spectrum[1]

    def spread(stacked):
        return lax.all_to_all(stacked, "seq", split_axis=3, concat_axis=2, tiled=True)

    def collect(twisted):
        return lax.all_to_all(twisted, "seq", split_axis=4, concat_axis=3, tiled=True)

    def deliver(untwisted):
        return lax.all_to_all(untwisted, "seq", split_axis=4, concat_axis=3, tiled=True)

    def restore(values):
        return lax.all_to_all(values, "seq", split_axis=2, concat_axis=3, tiled=True)

    forward_re, forward_im = transform(mixed_input[None], spread, collect, tables, location, length)
    forward_re = forward_re[0]
    forward_im = forward_im[0]
    output_re, output_im = forward_product(forward_re, forward_im, kernel_re, kernel_im)
    long_output = inverse(
        output_re[None], output_im[None], deliver, restore, tables, location, length
    )[0]
    backward_re, backward_im = transform(
        gated_cotangent[None], spread, collect, tables, location, length
    )
    backward_re = backward_re[0]
    backward_im = backward_im[0]
    input_re, input_im = backward_product(backward_re, backward_im, kernel_re, kernel_im)
    mixed_gradient = inverse(
        input_re[None], input_im[None], deliver, restore, tables, location, length
    )[0]
    front_re = grouped(forward_re, kernel_re)
    front_im = grouped(forward_im, kernel_re)
    back_re = grouped(backward_re, kernel_re)
    back_im = grouped(backward_im, kernel_re)
    filter_re = jnp.sum(front_re * back_re + front_im * back_im, axis=0) / length
    filter_im = jnp.sum(front_re * back_im - front_im * back_re, axis=0) / length
    gradient_filter = lax.psum(
        jnp.stack([filter_re, filter_im]).astype(jnp.bfloat16), "chan"
    ).astype(jnp.float32)
    long_values = long_output.reshape(channels, positions).astype(jnp.float32)
    mixed_values = mixed_gradient.reshape(channels, positions).astype(jnp.float32)
    output = (outer_gate.astype(jnp.float32) * long_values).astype(jnp.bfloat16)
    gradient_outer = (cotangent.astype(jnp.float32) * long_values).astype(jnp.bfloat16)
    gradient_inner = (mixed_values * signal.astype(jnp.float32)).astype(jnp.bfloat16)
    gradient_signal = (mixed_values * inner_gate.astype(jnp.float32)).astype(jnp.bfloat16)
    return (output, gradient_outer, gradient_inner, gradient_signal, gradient_filter)


def channel_slots(channels, filters, devices):
    if channels % devices or devices % filters:
        return 0
    return devices // filters


def pack_kernel(filters, rows, outer_ref, inner_ref, signal_ref, cotangent_ref, send_ref):
    factor = send_ref.shape[-1]
    products = (
        inner_ref[...].astype(jnp.float32) * signal_ref[...].astype(jnp.float32),
        cotangent_ref[...].astype(jnp.float32) * outer_ref[...].astype(jnp.float32),
    )
    for which, values in enumerate(products):
        pieces = jnp.stack([values[:, factor * r : factor * (r + 1)] for r in range(rows)], axis=0)
        turned = jnp.transpose(pieces, (1, 0, 2)).astype(jnp.bfloat16)
        for c in range(turned.shape[0]):
            send_ref[c % filters, 0, c // filters, which] = turned[c]


def unpack_kernel(
    filters, rows, back_ref, outer_ref, inner_ref, signal_ref, cotangent_ref, out_ref, d_outer, d_inner, d_signal
):
    factor = back_ref.shape[-1]
    count = outer_ref.shape[0]
    targets = (((out_ref, outer_ref), (d_outer, cotangent_ref)), ((d_inner, signal_ref), (d_signal, inner_ref)))
    for which, pairs in enumerate(targets):
        turned = jnp.stack(
            [back_ref[c % filters, 0, c // filters, which].astype(jnp.float32) for c in range(count)], axis=0
        )
        pieces = jnp.transpose(turned, (1, 0, 2))
        for r in range(rows):
            columns = slice(factor * r, factor * (r + 1))
            for target, gate in pairs:
                target[:, columns] = (gate[:, columns].astype(jnp.float32) * pieces[r]).astype(jnp.bfloat16)


def convolve_kernel(
    devices,
    shares,
    send_ref,
    taps_ref,
    cs_ref,
    ahead_ref,
    behind_ref,
    last_ref,
    wave_cos_ref,
    wave_sin_ref,
    back_ref,
    grads_ref,
    held,
    made,
    taps,
    grads,
    grads_sent,
    straight,
    filtered,
    unwound,
    send_sems,
    recv_sems,
    back_send_sems,
    back_recv_sems,
    small_send_sems,
    small_recv_sems,
):
    me = lax.axis_index("seq")
    count, rows, factor = send_ref.shape[1], send_ref.shape[3], send_ref.shape[4]
    step = held.shape[0] // 2 * rows
    length = factor * factor

    def peer(offset):
        return lax.rem(me + offset, devices)

    def copy(source, target, offset, send_sem, recv_sem):
        return pltpu.make_async_remote_copy(
            src_ref=source,
            dst_ref=target,
            send_sem=send_sem,
            recv_sem=recv_sem,
            device_id={"seq": peer(offset)},
            device_id_type=MESH,
        )

    def own(source, target, sem):
        return pltpu.make_async_copy(source, target, sem)

    def forth(offset, c):
        source = send_ref.at[peer(offset), c]
        if offset == 0:
            return own(source, held.at[me, c], recv_sems.at[0, c])
        return copy(source, held.at[me, c], offset, send_sems.at[offset, c], recv_sems.at[offset, c])

    def back(offset, c):
        source = made.at[c, peer(offset)]
        if offset == 0:
            return own(source, back_ref.at[me, c], back_recv_sems.at[0, c])
        return copy(source, back_ref.at[me, c], offset, back_send_sems.at[offset, c], back_recv_sems.at[offset, c])

    def tap(offset):
        source = taps_ref.at[peer(offset) // shares]
        if offset == 0:
            return own(source, taps.at[me], small_recv_sems.at[0, 0])
        return copy(source, taps.at[me], offset, small_send_sems.at[0, offset], small_recv_sems.at[0, offset])

    def grad(offset):
        source = grads_sent.at[peer(offset)]
        if offset == 0:
            return own(source, grads_ref.at[me], small_recv_sems.at[1, 0])
        return copy(source, grads_ref.at[me], offset, small_send_sems.at[1, offset], small_recv_sems.at[1, offset])

    order = [0] + [k for pair in zip(range(1, devices), range(devices - 1, 0, -1)) for k in pair][: devices - 1]

    barrier = pltpu.get_barrier_semaphore()
    for offset in range(1, devices):
        pl.semaphore_signal(barrier, inc=1, device_id={"seq": peer(offset)}, device_id_type=MESH)
    pl.semaphore_wait(barrier, devices - 1)

    for offset in order:
        tap(offset).start()

    @pl.loop(0, count)
    def _(c):
        for offset in order:
            forth(offset, c).start()

    grads[...] = jnp.zeros_like(grads)
    for offset in order:
        if offset == 0:
            tap(offset).wait()
        else:
            tap(offset).wait_recv()

    def dot(left, right):
        return jnp.dot(left, right, preferred_element_type=jnp.float32)

    @pl.loop(0, count)
    def _(c):
        for offset in order:
            if offset == 0:
                forth(offset, c).wait()
            else:
                forth(offset, c).wait_recv()

        @pl.loop(0, 2)
        def _(half):
            span = pl.ds(pl.multiple_of(half * step, step), step)
            low = pl.ds(pl.multiple_of(factor + half * step, step), step)
            wave_cos = wave_cos_ref[span, :]
            wave_sin = wave_sin_ref[span, :]
            spectra = []
            for which in range(2):
                source = held[:, c, which].reshape(factor, factor)
                p = dot(cs_ref[span, :], source)
                q = dot(cs_ref[low, :], source)
                straight[which, :, :factor] = (p * wave_cos - q * wave_sin).astype(jnp.bfloat16)
                straight[which, :, factor:] = (-q * wave_cos - p * wave_sin).astype(jnp.bfloat16)
            for which in range(2):
                spectrum = dot(straight[which], ahead_ref[...])
                spectra.append((spectrum[:, :factor], spectrum[:, factor:]))
            quarter = held.shape[0] // 2
            blocks = pl.ds(half * quarter, quarter)
            tap_re = taps[blocks, 0].reshape(step, factor).astype(jnp.float32)
            tap_im = taps[blocks, 1].reshape(step, factor).astype(jnp.float32)
            (f_re, f_im), (b_re, b_im) = spectra
            grads[0, span, :] += f_re * b_re + f_im * b_im
            grads[1, span, :] += f_re * b_im - f_im * b_re
            filtered[0, :, :factor] = (f_re * tap_re - f_im * tap_im).astype(jnp.bfloat16)
            filtered[0, :, factor:] = (f_re * tap_im + f_im * tap_re).astype(jnp.bfloat16)
            filtered[1, :, :factor] = (tap_re * b_re + tap_im * b_im).astype(jnp.bfloat16)
            filtered[1, :, factor:] = (tap_re * b_im - tap_im * b_re).astype(jnp.bfloat16)
            for which in range(2):
                values = dot(filtered[which], behind_ref[...])
                u_re, u_im = values[:, :factor], values[:, factor:]
                unwound[which, span, :] = (u_re * wave_cos - u_im * wave_sin).astype(jnp.bfloat16)
                unwound[which, low, :] = (u_im * wave_cos + u_re * wave_sin).astype(jnp.bfloat16)

        for which in range(2):
            values = (dot(last_ref[...], unwound[which]) * (1.0 / length)).astype(jnp.bfloat16)
            made[c, :, which] = values.reshape(devices, rows, factor)
        for offset in order:
            back(offset, c).start()

    for part in range(2):
        scaled = (grads[part] * (1.0 / length)).astype(jnp.bfloat16)
        grads_sent[:, part] = scaled.reshape(devices, rows, factor)
    for offset in order:
        grad(offset).start()
    for offset in order:
        if offset == 0:
            grad(offset).wait()
        else:
            grad(offset).wait()
            tap(offset).wait_send()

    @pl.loop(0, count)
    def _(c):
        for offset in order:
            if offset == 0:
                back(offset, c).wait()
            else:
                forth(offset, c).wait_send()
                back(offset, c).wait()


def by_channels(devices, shares, outer_gate, inner_gate, signal, filter_spectrum, cotangent):
    channels, positions = signal.shape
    filters, factor = filter_spectrum.shape[1], filter_spectrum.shape[3]
    rows = positions // factor
    count = channels // devices
    length = factor * factor
    block, depth = 16, 16
    per = block // filters
    split = count // per
    line = pl.BlockSpec((block, depth * factor), lambda i, t: (i, t))
    boxes = pl.BlockSpec(
        (filters, 1, per, 2, depth, factor), lambda i, t: (0, i // split, i % split, 0, t, 0)
    )
    grid = (channels // block, rows // depth)
    box_shape = (filters, shares, count, 2, rows, factor)
    limit = pltpu.CompilerParams(vmem_limit_bytes=VMEM_BYTES)
    send = pl.pallas_call(
        functools.partial(pack_kernel, filters, depth),
        grid=grid,
        in_specs=[line] * 4,
        out_specs=boxes,
        out_shape=jax.ShapeDtypeStruct(box_shape, jnp.bfloat16),
        compiler_params=limit,
        name="pack",
    )(outer_gate, inner_gate, signal, cotangent)
    send = send.reshape(devices, count, 2, rows, factor)
    cos_table, sin_table = wave_tables(factor)
    ordinal = jnp.arange(factor, dtype=jnp.int32)
    wave_cos, wave_sin = twist_grid(ordinal, ordinal, length)
    cs = jnp.concatenate([cos_table, sin_table], axis=0)
    ahead = jnp.block([[cos_table, -sin_table], [sin_table, cos_table]])
    behind = jnp.block([[cos_table, sin_table], [-sin_table, cos_table]])
    last = jnp.concatenate([cos_table, -sin_table], axis=1)
    taps = filter_spectrum.astype(jnp.bfloat16).transpose(1, 0, 2, 3)
    anywhere = pl.BlockSpec(memory_space=pl.ANY)
    inside = pl.BlockSpec(memory_space=pltpu.VMEM)
    back, grads = pl.pallas_call(
        functools.partial(convolve_kernel, devices, shares),
        in_specs=[anywhere, anywhere] + [inside] * 6,
        out_specs=[anywhere, anywhere],
        out_shape=[
            jax.ShapeDtypeStruct((devices, count, 2, rows, factor), jnp.bfloat16),
            jax.ShapeDtypeStruct((devices, 2, rows, factor), jnp.bfloat16),
        ],
        scratch_shapes=[
            pltpu.VMEM((devices, count, 2, rows, factor), jnp.bfloat16),
            pltpu.VMEM((count, devices, 2, rows, factor), jnp.bfloat16),
            pltpu.VMEM((devices, 2, rows, factor), jnp.bfloat16),
            pltpu.VMEM((2, factor, factor), jnp.float32),
            pltpu.VMEM((devices, 2, rows, factor), jnp.bfloat16),
            pltpu.VMEM((2, factor // 2, 2 * factor), jnp.bfloat16),
            pltpu.VMEM((2, factor // 2, 2 * factor), jnp.bfloat16),
            pltpu.VMEM((2, 2 * factor, factor), jnp.bfloat16),
            pltpu.SemaphoreType.DMA((devices, count)),
            pltpu.SemaphoreType.DMA((devices, count)),
            pltpu.SemaphoreType.DMA((devices, count)),
            pltpu.SemaphoreType.DMA((devices, count)),
            pltpu.SemaphoreType.DMA((2, devices)),
            pltpu.SemaphoreType.DMA((2, devices)),
        ],
        compiler_params=pltpu.CompilerParams(
            collective_id=0, has_side_effects=True, vmem_limit_bytes=VMEM_BYTES
        ),
        name="convolve",
    )(send, taps, cs, ahead, behind, last, wave_cos, wave_sin)
    shared = grads.astype(jnp.float32).reshape(filters, shares, 2, rows, factor).sum(axis=1)
    gradient_filter = lax.psum(
        shared.transpose(1, 0, 2, 3).astype(jnp.bfloat16), "chan"
    ).astype(jnp.float32)
    outputs = pl.pallas_call(
        functools.partial(unpack_kernel, filters, depth),
        grid=grid,
        in_specs=[boxes] + [line] * 4,
        out_specs=[line] * 4,
        out_shape=[jax.ShapeDtypeStruct((channels, positions), jnp.bfloat16)] * 4,
        compiler_params=limit,
        name="unpack",
    )(back.reshape(box_shape), outer_gate, inner_gate, signal, cotangent)
    return (*outputs, gradient_filter)


def local_program(devices, outer_gate, inner_gate, signal, filter_spectrum, cotangent):
    filters = filter_spectrum.shape[1]
    shares = channel_slots(signal.shape[0], filters, devices)
    program = functools.partial(by_channels, devices, shares) if shares else per_device
    return program(outer_gate, inner_gate, signal, filter_spectrum, cotangent)


def solution(mesh):
    in_specs = (
        P("chan", "seq"),
        P("chan", "seq"),
        P("chan", "seq"),
        P(None, None, "seq", None),
        P("chan", "seq"),
    )
    out_specs = (
        P("chan", "seq"),
        P("chan", "seq"),
        P("chan", "seq"),
        P("chan", "seq"),
        P(None, None, "seq", None),
    )
    return jax.shard_map(
        functools.partial(local_program, mesh.shape["seq"]), mesh=mesh, in_specs=in_specs, out_specs=out_specs, check_vma=False
    )
```

```python
import functools
import math

import jax
import jax.numpy as jnp
import numpy as np
from jax import lax
from jax.experimental import pallas as pl
from jax.experimental.pallas import tpu as pltpu
from jax.sharding import PartitionSpec as P

MESH = pl.DeviceIdType.MESH
VMEM_BYTES = 56 * 1024 * 1024


def wave_tables(factor):
    ordinal = jnp.arange(factor, dtype=jnp.int32)
    phases = ordinal[:, None] * ordinal[None, :] % factor
    angles = phases.astype(jnp.float32) * (2.0 * math.pi / factor)
    return (jnp.cos(angles).astype(jnp.bfloat16), jnp.sin(angles).astype(jnp.bfloat16))


def twist_grid(leading, second, length):
    phases = leading[:, None] * second[None, :] % length
    angles = phases.astype(jnp.float32) * (2.0 * math.pi / length)
    return (jnp.cos(angles), jnp.sin(angles))


def product(operand, pattern, matrix):
    return jnp.einsum(pattern, operand, matrix, preferred_element_type=jnp.float32)


def transform(stacked, spread, collect, tables, location, length):
    cos_table, sin_table = tables
    factor = cos_table.shape[0]
    received = spread(stacked)
    block_size = received.shape[3]
    columns = location * block_size + jnp.arange(block_size, dtype=jnp.int32)
    wave_cos, wave_sin = twist_grid(columns, jnp.arange(factor, dtype=jnp.int32), length)
    sectioned_re = product(received, "ncab,ak->ncbk", cos_table)
    sectioned_im = -product(received, "ncab,ak->ncbk", sin_table)
    twisted = jnp.stack(
        [
            sectioned_re * wave_cos + sectioned_im * wave_sin,
            sectioned_im * wave_cos - sectioned_re * wave_sin,
        ],
        axis=1,
    ).astype(jnp.bfloat16)
    arrived = collect(twisted)
    arrived_re = arrived[:, 0]
    arrived_im = arrived[:, 1]
    spectrum_re = product(arrived_re, "ncbk,bm->nckm", cos_table) + product(
        arrived_im, "ncbk,bm->nckm", sin_table
    )
    spectrum_im = product(arrived_im, "ncbk,bm->nckm", cos_table) - product(
        arrived_re, "ncbk,bm->nckm", sin_table
    )
    return (spectrum_re, spectrum_im)


def inverse(spectrum_re, spectrum_im, deliver, restore, tables, location, length):
    cos_table, sin_table = tables
    factor = cos_table.shape[0]
    shrink = 1.0 / factor
    block_size = spectrum_re.shape[2]
    row_ids = location * block_size + jnp.arange(block_size, dtype=jnp.int32)
    wave_cos, wave_sin = twist_grid(row_ids, jnp.arange(factor, dtype=jnp.int32), length)
    unwound_re = (
        product(spectrum_re, "nckm,mb->nckb", cos_table)
        - product(spectrum_im, "nckm,mb->nckb", sin_table)
    ) * shrink
    unwound_im = (
        product(spectrum_im, "nckm,mb->nckb", cos_table)
        + product(spectrum_re, "nckm,mb->nckb", sin_table)
    ) * shrink
    untwisted = jnp.stack(
        [
            unwound_re * wave_cos - unwound_im * wave_sin,
            unwound_im * wave_cos + unwound_re * wave_sin,
        ],
        axis=1,
    ).astype(jnp.bfloat16)
    arrived = deliver(untwisted)
    values = (
        (
            product(arrived[:, 0], "nckb,ka->ncab", cos_table)
            - product(arrived[:, 1], "nckb,ka->ncab", sin_table)
        )
        * shrink
    ).astype(jnp.bfloat16)
    return restore(values)


def grouped(values, kernel):
    return values.reshape((-1,) + kernel.shape)


def forward_product(forward_re, forward_im, kernel_re, kernel_im):
    shape = forward_re.shape
    front_re = grouped(forward_re, kernel_re)
    front_im = grouped(forward_im, kernel_re)
    output_re = (front_re * kernel_re - front_im * kernel_im).astype(jnp.bfloat16).reshape(shape)
    output_im = (front_re * kernel_im + front_im * kernel_re).astype(jnp.bfloat16).reshape(shape)
    return (output_re, output_im)


def backward_product(backward_re, backward_im, kernel_re, kernel_im):
    shape = backward_re.shape
    back_re = grouped(backward_re, kernel_re)
    back_im = grouped(backward_im, kernel_re)
    input_re = (kernel_re * back_re + kernel_im * back_im).astype(jnp.bfloat16).reshape(shape)
    input_im = (kernel_re * back_im - kernel_im * back_re).astype(jnp.bfloat16).reshape(shape)
    return (input_re, input_im)


def per_device(outer_gate, inner_gate, signal, filter_spectrum, cotangent):
    channels, positions = signal.shape
    factor = filter_spectrum.shape[3]
    length = factor * factor
    row_count = positions // factor
    location = lax.axis_index("seq")
    tables = wave_tables(factor)
    mixed_input = (
        (inner_gate.astype(jnp.float32) * signal.astype(jnp.float32))
        .astype(jnp.bfloat16)
        .reshape(channels, row_count, factor)
    )
    gated_cotangent = (
        (cotangent.astype(jnp.float32) * outer_gate.astype(jnp.float32))
        .astype(jnp.bfloat16)
        .reshape(channels, row_count, factor)
    )
    kernel_re = filter_spectrum[0]
    kernel_im = filter_spectrum[1]

    def spread(stacked):
        return lax.all_to_all(stacked, "seq", split_axis=3, concat_axis=2, tiled=True)

    def collect(twisted):
        return lax.all_to_all(twisted, "seq", split_axis=4, concat_axis=3, tiled=True)

    def deliver(untwisted):
        return lax.all_to_all(untwisted, "seq", split_axis=4, concat_axis=3, tiled=True)

    def restore(values):
        return lax.all_to_all(values, "seq", split_axis=2, concat_axis=3, tiled=True)

    forward_re, forward_im = transform(mixed_input[None], spread, collect, tables, location, length)
    forward_re = forward_re[0]
    forward_im = forward_im[0]
    output_re, output_im = forward_product(forward_re, forward_im, kernel_re, kernel_im)
    long_output = inverse(
        output_re[None], output_im[None], deliver, restore, tables, location, length
    )[0]
    backward_re, backward_im = transform(
        gated_cotangent[None], spread, collect, tables, location, length
    )
    backward_re = backward_re[0]
    backward_im = backward_im[0]
    input_re, input_im = backward_product(backward_re, backward_im, kernel_re, kernel_im)
    mixed_gradient = inverse(
        input_re[None], input_im[None], deliver, restore, tables, location, length
    )[0]
    front_re = grouped(forward_re, kernel_re)
    front_im = grouped(forward_im, kernel_re)
    back_re = grouped(backward_re, kernel_re)
    back_im = grouped(backward_im, kernel_re)
    filter_re = jnp.sum(front_re * back_re + front_im * back_im, axis=0) / length
    filter_im = jnp.sum(front_re * back_im - front_im * back_re, axis=0) / length
    gradient_filter = lax.psum(
        jnp.stack([filter_re, filter_im]).astype(jnp.bfloat16), "chan"
    ).astype(jnp.float32)
    long_values = long_output.reshape(channels, positions).astype(jnp.float32)
    mixed_values = mixed_gradient.reshape(channels, positions).astype(jnp.float32)
    output = (outer_gate.astype(jnp.float32) * long_values).astype(jnp.bfloat16)
    gradient_outer = (cotangent.astype(jnp.float32) * long_values).astype(jnp.bfloat16)
    gradient_inner = (mixed_values * signal.astype(jnp.float32)).astype(jnp.bfloat16)
    gradient_signal = (mixed_values * inner_gate.astype(jnp.float32)).astype(jnp.bfloat16)
    return (output, gradient_outer, gradient_inner, gradient_signal, gradient_filter)


def channel_slots(channels, filters, devices, rows, lanes):
    if channels % devices or devices % filters or devices % 2 or channels % 16 or 16 % filters:
        return 0
    if (channels // devices) % (16 // filters) or rows % (16 * lanes):
        return 0
    return devices // filters


def pack_kernel(filters, rows, outer_ref, inner_ref, signal_ref, cotangent_ref, send_ref):
    factor = send_ref.shape[-1]
    products = (
        inner_ref[...].astype(jnp.float32) * signal_ref[...].astype(jnp.float32),
        cotangent_ref[...].astype(jnp.float32) * outer_ref[...].astype(jnp.float32),
    )
    for which, values in enumerate(products):
        pieces = jnp.stack([values[:, factor * r : factor * (r + 1)] for r in range(rows)], axis=0)
        turned = jnp.transpose(pieces, (1, 0, 2)).astype(jnp.bfloat16)
        for c in range(turned.shape[0]):
            send_ref[c % filters, 0, c // filters, which] = turned[c]


def unpack_kernel(
    filters, rows, back_ref, outer_ref, inner_ref, signal_ref, cotangent_ref, out_ref, d_outer, d_inner, d_signal
):
    factor = back_ref.shape[-1]
    count = outer_ref.shape[0]
    targets = (((out_ref, outer_ref), (d_outer, cotangent_ref)), ((d_inner, signal_ref), (d_signal, inner_ref)))
    for which, pairs in enumerate(targets):
        turned = jnp.stack(
            [back_ref[c % filters, 0, c // filters, which].astype(jnp.float32) for c in range(count)], axis=0
        )
        pieces = jnp.transpose(turned, (1, 0, 2))
        for r in range(rows):
            columns = slice(factor * r, factor * (r + 1))
            for target, gate in pairs:
                target[:, columns] = (gate[:, columns].astype(jnp.float32) * pieces[r]).astype(jnp.bfloat16)


def convolve_kernel(
    devices,
    lanes,
    shares,
    send_ref,
    taps_ref,
    cs_ref,
    ahead_ref,
    behind_ref,
    last_ref,
    wave_cos_ref,
    wave_sin_ref,
    back_ref,
    grads_ref,
    held,
    made,
    taps,
    grads,
    grads_sent,
    parts,
    quarter,
    arrived,
    merged,
    total,
    straight,
    filtered,
    unwound,
    send_sems,
    recv_sems,
    back_send_sems,
    back_recv_sems,
    small_send_sems,
    small_recv_sems,
    lane_send_sems,
    lane_recv_sems,
):
    me = lax.axis_index("seq")
    lane = lax.axis_index("chan")
    count, rows, factor = send_ref.shape[1], send_ref.shape[3], send_ref.shape[4]
    step = held.shape[0] // 2 * rows
    length = factor * factor
    thin = rows // lanes

    def peer(offset):
        return lax.rem(me + offset, devices)

    def lane_peer(offset):
        return lax.rem(lane + offset, lanes)

    def thin_rows(which):
        return pl.ds(pl.multiple_of(which * thin, thin), thin)

    def across(source, target, stage, offset):
        if offset == 0:
            return pltpu.make_async_copy(source, target, lane_recv_sems.at[stage, 0])
        return pltpu.make_async_remote_copy(
            src_ref=source,
            dst_ref=target,
            send_sem=lane_send_sems.at[stage, offset],
            recv_sem=lane_recv_sems.at[stage, offset],
            device_id={"chan": lane_peer(offset)},
            device_id_type=MESH,
        )

    def taps_across(offset):
        mine = taps.at[:, :, thin_rows(lane), :]
        return across(mine, mine, 0, offset)

    def parts_across(offset):
        return across(grads_sent.at[:, :, thin_rows(lane_peer(offset)), :], parts.at[lane], 1, offset)

    def merged_across(offset):
        return across(merged, total.at[lane], 2, offset)

    def arrive(make, offset):
        if offset == 0:
            make(offset).wait()
        else:
            make(offset).wait_recv()

    def copy(source, target, offset, send_sem, recv_sem):
        return pltpu.make_async_remote_copy(
            src_ref=source,
            dst_ref=target,
            send_sem=send_sem,
            recv_sem=recv_sem,
            device_id={"seq": peer(offset)},
            device_id_type=MESH,
        )

    def own(source, target, sem):
        return pltpu.make_async_copy(source, target, sem)

    def forth(offset, c):
        source = send_ref.at[peer(offset), c]
        if offset == 0:
            return own(source, held.at[me, c], recv_sems.at[0, c])
        return copy(source, held.at[me, c], offset, send_sems.at[offset, c], recv_sems.at[offset, c])

    def back(offset, c):
        source = made.at[c, peer(offset)]
        if offset == 0:
            return own(source, back_ref.at[me, c], back_recv_sems.at[0, c])
        return copy(source, back_ref.at[me, c], offset, back_send_sems.at[offset, c], back_recv_sems.at[offset, c])

    def tap(offset):
        source = taps_ref.at[peer(offset) // shares, :, thin_rows(lane), :]
        target = taps.at[me, :, thin_rows(lane), :]
        if offset == 0:
            return own(source, target, small_recv_sems.at[0, 0])
        return copy(source, target, offset, small_send_sems.at[0, offset], small_recv_sems.at[0, offset])

    def grad(offset):
        source = quarter.at[peer(offset)]
        if offset == 0:
            return own(source, arrived.at[me], small_recv_sems.at[1, 0])
        return copy(source, arrived.at[me], offset, small_send_sems.at[1, offset], small_recv_sems.at[1, offset])

    order = [0] + [k for pair in zip(range(1, devices), range(devices - 1, 0, -1)) for k in pair][: devices - 1]

    barrier = pltpu.get_barrier_semaphore()
    for offset in range(1, devices):
        pl.semaphore_signal(barrier, inc=1, device_id={"seq": peer(offset)}, device_id_type=MESH)
    for offset in range(1, lanes):
        pl.semaphore_signal(barrier, inc=1, device_id={"chan": lane_peer(offset)}, device_id_type=MESH)
    pl.semaphore_wait(barrier, devices + lanes - 2)

    def start_all(make, first, end):
        @pl.loop(first, end)
        def _(c):
            for offset in order:
                make(offset, c).start()

    marks = (count // 4, count * 5 // 8, count * 7 // 8)
    for offset in order:
        tap(offset).start()
    start_all(forth, 0, marks[0])
    for offset in order:
        arrive(tap, offset)
    for offset in range(1, lanes):
        taps_across(offset).start()
    start_all(forth, marks[0], count)
    grads[...] = jnp.zeros_like(grads)
    for offset in range(1, lanes):
        taps_across(offset).wait_recv()

    def dot(left, right):
        return jnp.dot(left, right, preferred_element_type=jnp.float32)

    @pl.loop(0, count)
    def _(c):
        @pl.when(c == count - 1)
        def _():
            start_all(back, 0, marks[0])

        for offset in order:
            arrive(lambda o: forth(o, c), offset)

        @pl.loop(0, 2)
        def _(half):
            span = pl.ds(pl.multiple_of(half * step, step), step)
            low = pl.ds(pl.multiple_of(factor + half * step, step), step)
            wave_cos = wave_cos_ref[span, :]
            wave_sin = wave_sin_ref[span, :]
            spectra = []
            for which in range(2):
                source = held[:, c, which].reshape(factor, factor)
                p = dot(cs_ref[span, :], source)
                q = dot(cs_ref[low, :], source)
                straight[which, :, :factor] = (p * wave_cos - q * wave_sin).astype(jnp.bfloat16)
                straight[which, :, factor:] = (-q * wave_cos - p * wave_sin).astype(jnp.bfloat16)
            for which in range(2):
                spectrum = dot(straight[which], ahead_ref[...])
                spectra.append((spectrum[:, :factor], spectrum[:, factor:]))
            quarter = held.shape[0] // 2
            blocks = pl.ds(half * quarter, quarter)
            tap_re = taps[blocks, 0].reshape(step, factor).astype(jnp.float32)
            tap_im = taps[blocks, 1].reshape(step, factor).astype(jnp.float32)
            (f_re, f_im), (b_re, b_im) = spectra
            grads[0, span, :] += f_re * b_re + f_im * b_im
            grads[1, span, :] += f_re * b_im - f_im * b_re
            filtered[0, :, :factor] = (f_re * tap_re - f_im * tap_im).astype(jnp.bfloat16)
            filtered[0, :, factor:] = (f_re * tap_im + f_im * tap_re).astype(jnp.bfloat16)
            filtered[1, :, :factor] = (tap_re * b_re + tap_im * b_im).astype(jnp.bfloat16)
            filtered[1, :, factor:] = (tap_re * b_im - tap_im * b_re).astype(jnp.bfloat16)
            for which in range(2):
                values = dot(filtered[which], behind_ref[...])
                u_re, u_im = values[:, :factor], values[:, factor:]
                unwound[which, span, :] = (u_re * wave_cos - u_im * wave_sin).astype(jnp.bfloat16)
                unwound[which, low, :] = (u_im * wave_cos + u_re * wave_sin).astype(jnp.bfloat16)

        for which in range(2):
            values = (dot(last_ref[...], unwound[which]) * (1.0 / length)).astype(jnp.bfloat16)
            made[c, :, which] = values.reshape(devices, rows, factor)

    for part in range(2):
        scaled = (grads[part] * (1.0 / length)).astype(jnp.bfloat16)
        grads_sent[:, part] = scaled.reshape(devices, rows, factor)
    for offset in range(lanes):
        parts_across(offset).start()
    start_all(back, marks[0], marks[1])
    for offset in range(lanes):
        arrive(parts_across, offset)
    summed = parts[0].astype(jnp.float32)
    for which in range(1, lanes):
        summed = summed + parts[which].astype(jnp.float32)
    quarter[...] = summed.astype(jnp.bfloat16)
    for offset in order:
        grad(offset).start()
    start_all(back, marks[1], marks[2])
    for offset in order:
        arrive(grad, offset)
    for group in range(devices // shares):
        summed = arrived[group * shares].astype(jnp.float32)
        for which in range(1, shares):
            summed = summed + arrived[group * shares + which].astype(jnp.float32)
        merged[group] = summed.astype(jnp.bfloat16)
    for offset in range(lanes):
        merged_across(offset).start()
    start_all(back, marks[2], count)
    for offset in range(lanes):
        arrive(merged_across, offset)
    for which in range(lanes):
        for part in range(2):
            grads_ref[part, :, which * thin : (which + 1) * thin, :] = total[which, :, part].astype(jnp.float32)
    for offset in range(1, lanes):
        for make in (taps_across, parts_across, merged_across):
            make(offset).wait_send()
    for offset in range(1, devices):
        for make in (tap, grad):
            make(offset).wait_send()

    @pl.loop(0, count)
    def _(c):
        for offset in order:
            if offset == 0:
                back(offset, c).wait()
            else:
                forth(offset, c).wait_send()
                back(offset, c).wait()


def wave_constants(factor):
    ordinal = np.arange(factor)
    angles = (np.outer(ordinal, ordinal) % factor) * (2.0 * np.pi / factor)
    cos_table, sin_table = np.cos(angles), np.sin(angles)
    twists = np.outer(ordinal, ordinal) * (2.0 * np.pi / (factor * factor))
    tables = (
        np.concatenate([cos_table, sin_table], axis=0),
        np.block([[cos_table, -sin_table], [sin_table, cos_table]]),
        np.block([[cos_table, sin_table], [-sin_table, cos_table]]),
        np.concatenate([cos_table, -sin_table], axis=1),
    )
    return [t.astype(jnp.bfloat16) for t in tables] + [f(twists).astype(np.float32) for f in (np.cos, np.sin)]


def by_channels(devices, lanes, shares, outer_gate, inner_gate, signal, filter_spectrum, cotangent):
    channels, positions = signal.shape
    filters, factor = filter_spectrum.shape[1], filter_spectrum.shape[3]
    rows = positions // factor
    count = channels // devices
    block, depth = 16, 16
    per = block // filters
    split = count // per
    line = pl.BlockSpec((block, depth * factor), lambda i, t: (i, t))
    boxes = pl.BlockSpec(
        (filters, 1, per, 2, depth, factor), lambda i, t: (0, i // split, i % split, 0, t, 0)
    )
    grid = (channels // block, rows // depth)
    box_shape = (filters, shares, count, 2, rows, factor)
    limit = pltpu.CompilerParams(vmem_limit_bytes=VMEM_BYTES)
    send = pl.pallas_call(
        functools.partial(pack_kernel, filters, depth),
        grid=grid,
        in_specs=[line] * 4,
        out_specs=boxes,
        out_shape=jax.ShapeDtypeStruct(box_shape, jnp.bfloat16),
        compiler_params=limit,
        name="pack",
    )(outer_gate, inner_gate, signal, cotangent)
    send = send.reshape(devices, count, 2, rows, factor)
    taps = filter_spectrum.astype(jnp.bfloat16).transpose(1, 0, 2, 3)
    anywhere = pl.BlockSpec(memory_space=pl.ANY)
    inside = pl.BlockSpec(memory_space=pltpu.VMEM)
    thin = rows // lanes
    back, gradient_filter = pl.pallas_call(
        functools.partial(convolve_kernel, devices, lanes, shares),
        in_specs=[anywhere, anywhere] + [inside] * 6,
        out_specs=[anywhere, inside],
        out_shape=[
            jax.ShapeDtypeStruct((devices, count, 2, rows, factor), jnp.bfloat16),
            jax.ShapeDtypeStruct(filter_spectrum.shape, jnp.float32),
        ],
        scratch_shapes=[
            pltpu.VMEM((devices, count, 2, rows, factor), jnp.bfloat16),
            pltpu.VMEM((count, devices, 2, rows, factor), jnp.bfloat16),
            pltpu.VMEM((devices, 2, rows, factor), jnp.bfloat16),
            pltpu.VMEM((2, factor, factor), jnp.float32),
            pltpu.VMEM((devices, 2, rows, factor), jnp.bfloat16),
            pltpu.VMEM((lanes, devices, 2, thin, factor), jnp.bfloat16),
            pltpu.VMEM((devices, 2, thin, factor), jnp.bfloat16),
            pltpu.VMEM((devices, 2, thin, factor), jnp.bfloat16),
            pltpu.VMEM((filters, 2, thin, factor), jnp.bfloat16),
            pltpu.VMEM((lanes, filters, 2, thin, factor), jnp.bfloat16),
            pltpu.VMEM((2, factor // 2, 2 * factor), jnp.bfloat16),
            pltpu.VMEM((2, factor // 2, 2 * factor), jnp.bfloat16),
            pltpu.VMEM((2, 2 * factor, factor), jnp.bfloat16),
            pltpu.SemaphoreType.DMA((devices, count)),
            pltpu.SemaphoreType.DMA((devices, count)),
            pltpu.SemaphoreType.DMA((devices, count)),
            pltpu.SemaphoreType.DMA((devices, count)),
            pltpu.SemaphoreType.DMA((2, devices)),
            pltpu.SemaphoreType.DMA((2, devices)),
            pltpu.SemaphoreType.DMA((3, lanes)),
            pltpu.SemaphoreType.DMA((3, lanes)),
        ],
        compiler_params=pltpu.CompilerParams(
            collective_id=0, has_side_effects=True, vmem_limit_bytes=VMEM_BYTES
        ),
        name="convolve",
    )(send, taps, *wave_constants(factor))
    outputs = pl.pallas_call(
        functools.partial(unpack_kernel, filters, depth),
        grid=grid,
        in_specs=[boxes] + [line] * 4,
        out_specs=[line] * 4,
        out_shape=[jax.ShapeDtypeStruct((channels, positions), jnp.bfloat16)] * 4,
        compiler_params=limit,
        name="unpack",
    )(back.reshape(box_shape), outer_gate, inner_gate, signal, cotangent)
    return (*outputs, gradient_filter)


def local_program(devices, lanes, outer_gate, inner_gate, signal, filter_spectrum, cotangent):
    filters = filter_spectrum.shape[1]
    rows = signal.shape[1] // filter_spectrum.shape[3]
    shares = channel_slots(signal.shape[0], filters, devices, rows, lanes)
    program = functools.partial(by_channels, devices, lanes, shares) if shares else per_device
    return program(outer_gate, inner_gate, signal, filter_spectrum, cotangent)


def solution(mesh):
    in_specs = (
        P("chan", "seq"),
        P("chan", "seq"),
        P("chan", "seq"),
        P(None, None, "seq", None),
        P("chan", "seq"),
    )
    out_specs = (
        P("chan", "seq"),
        P("chan", "seq"),
        P("chan", "seq"),
        P("chan", "seq"),
        P(None, None, "seq", None),
    )
    return jax.shard_map(
        functools.partial(local_program, mesh.shape["seq"], mesh.shape["chan"]), mesh=mesh, in_specs=in_specs, out_specs=out_specs, check_vma=False
    )
```

```python
import functools
import math

import jax
import jax.numpy as jnp
import numpy as np
from jax import lax
from jax.experimental import pallas as pl
from jax.experimental.pallas import tpu as pltpu
from jax.sharding import PartitionSpec as P

MESH = pl.DeviceIdType.MESH
VMEM_BYTES = 56 * 1024 * 1024


def wave_tables(factor):
    ordinal = jnp.arange(factor, dtype=jnp.int32)
    phases = ordinal[:, None] * ordinal[None, :] % factor
    angles = phases.astype(jnp.float32) * (2.0 * math.pi / factor)
    return (jnp.cos(angles).astype(jnp.bfloat16), jnp.sin(angles).astype(jnp.bfloat16))


def twist_grid(leading, second, length):
    phases = leading[:, None] * second[None, :] % length
    angles = phases.astype(jnp.float32) * (2.0 * math.pi / length)
    return (jnp.cos(angles), jnp.sin(angles))


def product(operand, pattern, matrix):
    return jnp.einsum(pattern, operand, matrix, preferred_element_type=jnp.float32)


def transform(stacked, spread, collect, tables, location, length):
    cos_table, sin_table = tables
    factor = cos_table.shape[0]
    received = spread(stacked)
    block_size = received.shape[3]
    columns = location * block_size + jnp.arange(block_size, dtype=jnp.int32)
    wave_cos, wave_sin = twist_grid(columns, jnp.arange(factor, dtype=jnp.int32), length)
    sectioned_re = product(received, "ncab,ak->ncbk", cos_table)
    sectioned_im = -product(received, "ncab,ak->ncbk", sin_table)
    twisted = jnp.stack(
        [
            sectioned_re * wave_cos + sectioned_im * wave_sin,
            sectioned_im * wave_cos - sectioned_re * wave_sin,
        ],
        axis=1,
    ).astype(jnp.bfloat16)
    arrived = collect(twisted)
    arrived_re = arrived[:, 0]
    arrived_im = arrived[:, 1]
    spectrum_re = product(arrived_re, "ncbk,bm->nckm", cos_table) + product(
        arrived_im, "ncbk,bm->nckm", sin_table
    )
    spectrum_im = product(arrived_im, "ncbk,bm->nckm", cos_table) - product(
        arrived_re, "ncbk,bm->nckm", sin_table
    )
    return (spectrum_re, spectrum_im)


def inverse(spectrum_re, spectrum_im, deliver, restore, tables, location, length):
    cos_table, sin_table = tables
    factor = cos_table.shape[0]
    shrink = 1.0 / factor
    block_size = spectrum_re.shape[2]
    row_ids = location * block_size + jnp.arange(block_size, dtype=jnp.int32)
    wave_cos, wave_sin = twist_grid(row_ids, jnp.arange(factor, dtype=jnp.int32), length)
    unwound_re = (
        product(spectrum_re, "nckm,mb->nckb", cos_table)
        - product(spectrum_im, "nckm,mb->nckb", sin_table)
    ) * shrink
    unwound_im = (
        product(spectrum_im, "nckm,mb->nckb", cos_table)
        + product(spectrum_re, "nckm,mb->nckb", sin_table)
    ) * shrink
    untwisted = jnp.stack(
        [
            unwound_re * wave_cos - unwound_im * wave_sin,
            unwound_im * wave_cos + unwound_re * wave_sin,
        ],
        axis=1,
    ).astype(jnp.bfloat16)
    arrived = deliver(untwisted)
    values = (
        (
            product(arrived[:, 0], "nckb,ka->ncab", cos_table)
            - product(arrived[:, 1], "nckb,ka->ncab", sin_table)
        )
        * shrink
    ).astype(jnp.bfloat16)
    return restore(values)


def grouped(values, kernel):
    return values.reshape((-1,) + kernel.shape)


def forward_product(forward_re, forward_im, kernel_re, kernel_im):
    shape = forward_re.shape
    front_re = grouped(forward_re, kernel_re)
    front_im = grouped(forward_im, kernel_re)
    output_re = (front_re * kernel_re - front_im * kernel_im).astype(jnp.bfloat16).reshape(shape)
    output_im = (front_re * kernel_im + front_im * kernel_re).astype(jnp.bfloat16).reshape(shape)
    return (output_re, output_im)


def backward_product(backward_re, backward_im, kernel_re, kernel_im):
    shape = backward_re.shape
    back_re = grouped(backward_re, kernel_re)
    back_im = grouped(backward_im, kernel_re)
    input_re = (kernel_re * back_re + kernel_im * back_im).astype(jnp.bfloat16).reshape(shape)
    input_im = (kernel_re * back_im - kernel_im * back_re).astype(jnp.bfloat16).reshape(shape)
    return (input_re, input_im)


def per_device(outer_gate, inner_gate, signal, filter_spectrum, cotangent):
    channels, positions = signal.shape
    factor = filter_spectrum.shape[3]
    length = factor * factor
    row_count = positions // factor
    location = lax.axis_index("seq")
    tables = wave_tables(factor)
    mixed_input = (
        (inner_gate.astype(jnp.float32) * signal.astype(jnp.float32))
        .astype(jnp.bfloat16)
        .reshape(channels, row_count, factor)
    )
    gated_cotangent = (
        (cotangent.astype(jnp.float32) * outer_gate.astype(jnp.float32))
        .astype(jnp.bfloat16)
        .reshape(channels, row_count, factor)
    )
    kernel_re = filter_spectrum[0]
    kernel_im = filter_spectrum[1]

    def spread(stacked):
        return lax.all_to_all(stacked, "seq", split_axis=3, concat_axis=2, tiled=True)

    def collect(twisted):
        return lax.all_to_all(twisted, "seq", split_axis=4, concat_axis=3, tiled=True)

    def deliver(untwisted):
        return lax.all_to_all(untwisted, "seq", split_axis=4, concat_axis=3, tiled=True)

    def restore(values):
        return lax.all_to_all(values, "seq", split_axis=2, concat_axis=3, tiled=True)

    forward_re, forward_im = transform(mixed_input[None], spread, collect, tables, location, length)
    forward_re = forward_re[0]
    forward_im = forward_im[0]
    output_re, output_im = forward_product(forward_re, forward_im, kernel_re, kernel_im)
    long_output = inverse(
        output_re[None], output_im[None], deliver, restore, tables, location, length
    )[0]
    backward_re, backward_im = transform(
        gated_cotangent[None], spread, collect, tables, location, length
    )
    backward_re = backward_re[0]
    backward_im = backward_im[0]
    input_re, input_im = backward_product(backward_re, backward_im, kernel_re, kernel_im)
    mixed_gradient = inverse(
        input_re[None], input_im[None], deliver, restore, tables, location, length
    )[0]
    front_re = grouped(forward_re, kernel_re)
    front_im = grouped(forward_im, kernel_re)
    back_re = grouped(backward_re, kernel_re)
    back_im = grouped(backward_im, kernel_re)
    filter_re = jnp.sum(front_re * back_re + front_im * back_im, axis=0) / length
    filter_im = jnp.sum(front_re * back_im - front_im * back_re, axis=0) / length
    gradient_filter = lax.psum(
        jnp.stack([filter_re, filter_im]).astype(jnp.bfloat16), "chan"
    ).astype(jnp.float32)
    long_values = long_output.reshape(channels, positions).astype(jnp.float32)
    mixed_values = mixed_gradient.reshape(channels, positions).astype(jnp.float32)
    output = (outer_gate.astype(jnp.float32) * long_values).astype(jnp.bfloat16)
    gradient_outer = (cotangent.astype(jnp.float32) * long_values).astype(jnp.bfloat16)
    gradient_inner = (mixed_values * signal.astype(jnp.float32)).astype(jnp.bfloat16)
    gradient_signal = (mixed_values * inner_gate.astype(jnp.float32)).astype(jnp.bfloat16)
    return (output, gradient_outer, gradient_inner, gradient_signal, gradient_filter)


def channel_slots(channels, filters, devices, rows, lanes):
    if channels % devices or devices % filters or devices % 2 or channels % 16 or 16 % filters:
        return 0
    if (channels // devices) % (16 // filters) or rows % (16 * lanes):
        return 0
    return devices // filters


def pack_kernel(filters, rows, outer_ref, inner_ref, signal_ref, cotangent_ref, send_ref):
    factor = send_ref.shape[-1]
    products = (
        inner_ref[...].astype(jnp.float32) * signal_ref[...].astype(jnp.float32),
        cotangent_ref[...].astype(jnp.float32) * outer_ref[...].astype(jnp.float32),
    )
    for which, values in enumerate(products):
        pieces = jnp.stack([values[:, factor * r : factor * (r + 1)] for r in range(rows)], axis=0)
        turned = jnp.transpose(pieces, (1, 0, 2)).astype(jnp.bfloat16)
        for c in range(turned.shape[0]):
            send_ref[c % filters, 0, c // filters, which] = turned[c]


def unpack_kernel(
    filters, rows, back_ref, outer_ref, inner_ref, signal_ref, cotangent_ref, out_ref, d_outer, d_inner, d_signal
):
    factor = back_ref.shape[-1]
    count = outer_ref.shape[0]
    targets = (((out_ref, outer_ref), (d_outer, cotangent_ref)), ((d_inner, signal_ref), (d_signal, inner_ref)))
    for which, pairs in enumerate(targets):
        turned = jnp.stack(
            [back_ref[c % filters, 0, c // filters, which].astype(jnp.float32) for c in range(count)], axis=0
        )
        pieces = jnp.transpose(turned, (1, 0, 2))
        for r in range(rows):
            columns = slice(factor * r, factor * (r + 1))
            for target, gate in pairs:
                target[:, columns] = (gate[:, columns].astype(jnp.float32) * pieces[r]).astype(jnp.bfloat16)


def convolve_kernel(
    devices,
    lanes,
    shares,
    send_ref,
    taps_ref,
    cs_far,
    ahead_far,
    behind_far,
    last_far,
    wave_cos_far,
    wave_sin_far,
    back_ref,
    grads_ref,
    held,
    made,
    taps,
    grads,
    grads_sent,
    parts,
    quarter,
    arrived,
    merged,
    total,
    straight,
    filtered,
    unwound,
    send_sems,
    recv_sems,
    back_send_sems,
    back_recv_sems,
    small_send_sems,
    small_recv_sems,
    lane_send_sems,
    lane_recv_sems,
    cs_ref,
    ahead_ref,
    behind_ref,
    last_ref,
    wave_cos_ref,
    wave_sin_ref,
    table_sems,
):
    me = lax.axis_index("seq")
    lane = lax.axis_index("chan")
    count, rows, factor = send_ref.shape[1], send_ref.shape[3], send_ref.shape[4]
    step = held.shape[0] // 2 * rows
    length = factor * factor
    thin = rows // lanes

    def peer(offset):
        return lax.rem(me + offset, devices)

    def lane_peer(offset):
        return lax.rem(lane + offset, lanes)

    def thin_rows(which):
        return pl.ds(pl.multiple_of(which * thin, thin), thin)

    def across(source, target, stage, offset):
        if offset == 0:
            return pltpu.make_async_copy(source, target, lane_recv_sems.at[stage, 0])
        return pltpu.make_async_remote_copy(
            src_ref=source,
            dst_ref=target,
            send_sem=lane_send_sems.at[stage, offset],
            recv_sem=lane_recv_sems.at[stage, offset],
            device_id={"chan": lane_peer(offset)},
            device_id_type=MESH,
        )

    def taps_across(offset):
        mine = taps.at[:, :, thin_rows(lane), :]
        return across(mine, mine, 0, offset)

    def parts_across(offset):
        return across(grads_sent.at[:, :, thin_rows(lane_peer(offset)), :], parts.at[lane], 1, offset)

    def merged_across(offset):
        return across(merged, total.at[lane], 2, offset)

    def arrive(make, offset):
        if offset == 0:
            make(offset).wait()
        else:
            make(offset).wait_recv()

    def copy(source, target, offset, send_sem, recv_sem):
        return pltpu.make_async_remote_copy(
            src_ref=source,
            dst_ref=target,
            send_sem=send_sem,
            recv_sem=recv_sem,
            device_id={"seq": peer(offset)},
            device_id_type=MESH,
        )

    def own(source, target, sem):
        return pltpu.make_async_copy(source, target, sem)

    def forth(offset, c):
        source = send_ref.at[peer(offset), c]
        if offset == 0:
            return own(source, held.at[me, c], recv_sems.at[0, c])
        return copy(source, held.at[me, c], offset, send_sems.at[offset, c], recv_sems.at[offset, c])

    def back(offset, c):
        source = made.at[c, peer(offset)]
        if offset == 0:
            return own(source, back_ref.at[me, c], back_recv_sems.at[0, c])
        return copy(source, back_ref.at[me, c], offset, back_send_sems.at[offset, c], back_recv_sems.at[offset, c])

    def tap(offset):
        source = taps_ref.at[peer(offset) // shares, :, thin_rows(lane), :]
        target = taps.at[me, :, thin_rows(lane), :]
        if offset == 0:
            return own(source, target, small_recv_sems.at[0, 0])
        return copy(source, target, offset, small_send_sems.at[0, offset], small_recv_sems.at[0, offset])

    def grad(offset):
        source = quarter.at[peer(offset)]
        if offset == 0:
            return own(source, arrived.at[me], small_recv_sems.at[1, 0])
        return copy(source, arrived.at[me], offset, small_send_sems.at[1, offset], small_recv_sems.at[1, offset])

    order = [0] + [k for pair in zip(range(1, devices), range(devices - 1, 0, -1)) for k in pair][: devices - 1]

    barrier = pltpu.get_barrier_semaphore()
    for offset in range(1, devices):
        pl.semaphore_signal(barrier, inc=1, device_id={"seq": peer(offset)}, device_id_type=MESH)
    for offset in range(1, lanes):
        pl.semaphore_signal(barrier, inc=1, device_id={"chan": lane_peer(offset)}, device_id_type=MESH)
    pl.semaphore_wait(barrier, devices + lanes - 2)

    def start_all(make, first, end):
        @pl.loop(first, end)
        def _(c):
            for offset in order:
                make(offset, c).start()

    marks = (count // 4, count * 5 // 8, count * 7 // 8)
    for offset in order:
        tap(offset).start()
    start_all(forth, 0, marks[0])
    far = (cs_far, ahead_far, behind_far, last_far, wave_cos_far, wave_sin_far)
    near = (cs_ref, ahead_ref, behind_ref, last_ref, wave_cos_ref, wave_sin_ref)
    tables = [own(source, target, table_sems.at[k]) for k, (source, target) in enumerate(zip(far, near))]
    for table in tables:
        table.start()
    for offset in order:
        arrive(tap, offset)
    for offset in range(1, lanes):
        taps_across(offset).start()
    start_all(forth, marks[0], count)
    grads[...] = jnp.zeros_like(grads)
    for offset in range(1, lanes):
        taps_across(offset).wait_recv()
    for table in tables:
        table.wait()

    def dot(left, right):
        return jnp.dot(left, right, preferred_element_type=jnp.float32)

    @pl.loop(0, count)
    def _(c):
        @pl.when(c == max(count - 2, marks[0]))
        def _():
            start_all(back, 0, marks[0])

        for offset in order:
            arrive(lambda o: forth(o, c), offset)

        @pl.loop(0, 2)
        def _(half):
            span = pl.ds(pl.multiple_of(half * step, step), step)
            low = pl.ds(pl.multiple_of(factor + half * step, step), step)
            wave_cos = wave_cos_ref[span, :]
            wave_sin = wave_sin_ref[span, :]
            spectra = []
            for which in range(2):
                source = held[:, c, which].reshape(factor, factor)
                p = dot(cs_ref[span, :], source)
                q = dot(cs_ref[low, :], source)
                straight[which, :, :factor] = (p * wave_cos - q * wave_sin).astype(jnp.bfloat16)
                straight[which, :, factor:] = (-q * wave_cos - p * wave_sin).astype(jnp.bfloat16)
            for which in range(2):
                spectrum = dot(straight[which], ahead_ref[...])
                spectra.append((spectrum[:, :factor], spectrum[:, factor:]))
            quarter = held.shape[0] // 2
            blocks = pl.ds(half * quarter, quarter)
            tap_re = taps[blocks, 0].reshape(step, factor).astype(jnp.float32)
            tap_im = taps[blocks, 1].reshape(step, factor).astype(jnp.float32)
            (f_re, f_im), (b_re, b_im) = spectra
            grads[0, span, :] += f_re * b_re + f_im * b_im
            grads[1, span, :] += f_re * b_im - f_im * b_re
            filtered[0, :, :factor] = (f_re * tap_re - f_im * tap_im).astype(jnp.bfloat16)
            filtered[0, :, factor:] = (f_re * tap_im + f_im * tap_re).astype(jnp.bfloat16)
            filtered[1, :, :factor] = (tap_re * b_re + tap_im * b_im).astype(jnp.bfloat16)
            filtered[1, :, factor:] = (tap_re * b_im - tap_im * b_re).astype(jnp.bfloat16)
            for which in range(2):
                values = dot(filtered[which], behind_ref[...])
                u_re, u_im = values[:, :factor], values[:, factor:]
                unwound[which, span, :] = (u_re * wave_cos - u_im * wave_sin).astype(jnp.bfloat16)
                unwound[which, low, :] = (u_im * wave_cos + u_re * wave_sin).astype(jnp.bfloat16)

        for which in range(2):
            values = (dot(last_ref[...], unwound[which]) * (1.0 / length)).astype(jnp.bfloat16)
            made[c, :, which] = values.reshape(devices, rows, factor)

    for part in range(2):
        scaled = (grads[part] * (1.0 / length)).astype(jnp.bfloat16)
        grads_sent[:, part] = scaled.reshape(devices, rows, factor)
    for offset in range(lanes):
        parts_across(offset).start()
    start_all(back, marks[0], marks[1])
    for offset in range(lanes):
        arrive(parts_across, offset)
    summed = parts[0].astype(jnp.float32)
    for which in range(1, lanes):
        summed = summed + parts[which].astype(jnp.float32)
    quarter[...] = summed.astype(jnp.bfloat16)
    for offset in order:
        grad(offset).start()
    start_all(back, marks[1], marks[2])
    for offset in order:
        arrive(grad, offset)
    for group in range(devices // shares):
        summed = arrived[group * shares].astype(jnp.float32)
        for which in range(1, shares):
            summed = summed + arrived[group * shares + which].astype(jnp.float32)
        merged[group] = summed.astype(jnp.bfloat16)
    for offset in range(lanes):
        merged_across(offset).start()
    start_all(back, marks[2], count)
    for offset in range(lanes):
        arrive(merged_across, offset)
    for which in range(lanes):
        for part in range(2):
            grads_ref[part, :, which * thin : (which + 1) * thin, :] = total[which, :, part].astype(jnp.float32)
    for offset in range(1, lanes):
        for make in (taps_across, parts_across, merged_across):
            make(offset).wait_send()
    for offset in range(1, devices):
        for make in (tap, grad):
            make(offset).wait_send()

    @pl.loop(0, count)
    def _(c):
        for offset in order:
            if offset == 0:
                back(offset, c).wait()
            else:
                forth(offset, c).wait_send()
                back(offset, c).wait()


def wave_constants(factor):
    ordinal = np.arange(factor)
    angles = (np.outer(ordinal, ordinal) % factor) * (2.0 * np.pi / factor)
    cos_table, sin_table = np.cos(angles), np.sin(angles)
    twists = np.outer(ordinal, ordinal) * (2.0 * np.pi / (factor * factor))
    tables = (
        np.concatenate([cos_table, sin_table], axis=0),
        np.block([[cos_table, -sin_table], [sin_table, cos_table]]),
        np.block([[cos_table, sin_table], [-sin_table, cos_table]]),
        np.concatenate([cos_table, -sin_table], axis=1),
    )
    return [t.astype(jnp.bfloat16) for t in tables] + [f(twists).astype(np.float32) for f in (np.cos, np.sin)]


def by_channels(devices, lanes, shares, outer_gate, inner_gate, signal, filter_spectrum, cotangent):
    channels, positions = signal.shape
    filters, factor = filter_spectrum.shape[1], filter_spectrum.shape[3]
    rows = positions // factor
    count = channels // devices
    block, depth = 16, 16
    per = block // filters
    split = count // per
    line = pl.BlockSpec((block, depth * factor), lambda i, t: (i, t))
    boxes = pl.BlockSpec(
        (filters, 1, per, 2, depth, factor), lambda i, t: (0, i // split, i % split, 0, t, 0)
    )
    grid = (channels // block, rows // depth)
    box_shape = (filters, shares, count, 2, rows, factor)
    limit = pltpu.CompilerParams(vmem_limit_bytes=VMEM_BYTES)
    send = pl.pallas_call(
        functools.partial(pack_kernel, filters, depth),
        grid=grid,
        in_specs=[line] * 4,
        out_specs=boxes,
        out_shape=jax.ShapeDtypeStruct(box_shape, jnp.bfloat16),
        compiler_params=limit,
        name="pack",
    )(outer_gate, inner_gate, signal, cotangent)
    send = send.reshape(devices, count, 2, rows, factor)
    taps = filter_spectrum.astype(jnp.bfloat16).transpose(1, 0, 2, 3)
    anywhere = pl.BlockSpec(memory_space=pl.ANY)
    inside = pl.BlockSpec(memory_space=pltpu.VMEM)
    thin = rows // lanes
    tables = wave_constants(factor)
    back, gradient_filter = pl.pallas_call(
        functools.partial(convolve_kernel, devices, lanes, shares),
        in_specs=[anywhere] * 8,
        out_specs=[anywhere, inside],
        out_shape=[
            jax.ShapeDtypeStruct((devices, count, 2, rows, factor), jnp.bfloat16),
            jax.ShapeDtypeStruct(filter_spectrum.shape, jnp.float32),
        ],
        scratch_shapes=[
            pltpu.VMEM((devices, count, 2, rows, factor), jnp.bfloat16),
            pltpu.VMEM((count, devices, 2, rows, factor), jnp.bfloat16),
            pltpu.VMEM((devices, 2, rows, factor), jnp.bfloat16),
            pltpu.VMEM((2, factor, factor), jnp.float32),
            pltpu.VMEM((devices, 2, rows, factor), jnp.bfloat16),
            pltpu.VMEM((lanes, devices, 2, thin, factor), jnp.bfloat16),
            pltpu.VMEM((devices, 2, thin, factor), jnp.bfloat16),
            pltpu.VMEM((devices, 2, thin, factor), jnp.bfloat16),
            pltpu.VMEM((filters, 2, thin, factor), jnp.bfloat16),
            pltpu.VMEM((lanes, filters, 2, thin, factor), jnp.bfloat16),
            pltpu.VMEM((2, factor // 2, 2 * factor), jnp.bfloat16),
            pltpu.VMEM((2, factor // 2, 2 * factor), jnp.bfloat16),
            pltpu.VMEM((2, 2 * factor, factor), jnp.bfloat16),
            pltpu.SemaphoreType.DMA((devices, count)),
            pltpu.SemaphoreType.DMA((devices, count)),
            pltpu.SemaphoreType.DMA((devices, count)),
            pltpu.SemaphoreType.DMA((devices, count)),
            pltpu.SemaphoreType.DMA((2, devices)),
            pltpu.SemaphoreType.DMA((2, devices)),
            pltpu.SemaphoreType.DMA((3, lanes)),
            pltpu.SemaphoreType.DMA((3, lanes)),
            *[pltpu.VMEM(table.shape, table.dtype) for table in tables],
            pltpu.SemaphoreType.DMA((len(tables),)),
        ],
        compiler_params=pltpu.CompilerParams(
            collective_id=0, has_side_effects=True, vmem_limit_bytes=VMEM_BYTES
        ),
        name="convolve",
    )(send, taps, *tables)
    outputs = pl.pallas_call(
        functools.partial(unpack_kernel, filters, depth),
        grid=grid,
        in_specs=[boxes] + [line] * 4,
        out_specs=[line] * 4,
        out_shape=[jax.ShapeDtypeStruct((channels, positions), jnp.bfloat16)] * 4,
        compiler_params=limit,
        name="unpack",
    )(back.reshape(box_shape), outer_gate, inner_gate, signal, cotangent)
    return (*outputs, gradient_filter)


def local_program(devices, lanes, outer_gate, inner_gate, signal, filter_spectrum, cotangent):
    filters = filter_spectrum.shape[1]
    rows = signal.shape[1] // filter_spectrum.shape[3]
    shares = channel_slots(signal.shape[0], filters, devices, rows, lanes)
    program = functools.partial(by_channels, devices, lanes, shares) if shares else per_device
    return program(outer_gate, inner_gate, signal, filter_spectrum, cotangent)


def solution(mesh):
    in_specs = (
        P("chan", "seq"),
        P("chan", "seq"),
        P("chan", "seq"),
        P(None, None, "seq", None),
        P("chan", "seq"),
    )
    out_specs = (
        P("chan", "seq"),
        P("chan", "seq"),
        P("chan", "seq"),
        P("chan", "seq"),
        P(None, None, "seq", None),
    )
    return jax.shard_map(
        functools.partial(local_program, mesh.shape["seq"], mesh.shape["chan"]), mesh=mesh, in_specs=in_specs, out_specs=out_specs, check_vma=False
    )
```
